256 devices in a mesh: grp: 2 (over core), gx: 16 (over z_hi, y), gy: 8 (over x, z_lo).
Axes of the slice: x: 4, y: 4, z: 8 (z_hi: 4, z_lo: 2; z = z_hi * 2 + z_lo), core: 2. Of those that a mesh axis runs over, the one named last changes fastest.
Arguments:
- source: bfloat16 [4, 128, 256, 1024], P(None, None, ('grp', 'gx'), 'gy'), may hold values from -6 to 6
- speed: bfloat16 [128, 256, 1024], P(('grp', 'gx'), None, 'gy'), may hold values from 1 to 2.5
- impedance: bfloat16 [128, 256, 1024], P(('grp', 'gx'), None, 'gy'), may hold values from 0.5 to 2
Outputs:
- pressure: float32 [128, 256, 1024], P(('grp', 'gx'), None, 'gy')
- velocity: float32 [3, 128, 256, 1024], P(None, ('grp', 'gx'), None, 'gy')
The draws below stay inside these ranges and needn't reach their ends.
All inputs are finite; a program needn't handle non-finite values.
Results may differ from the reference program's by a relative error of at most 0.0017.
Values may be sent and summed in bfloat16 or wider, within the bound.
A program may use at most 128 MiB of HBM per device.

```python
import math
import jax
import jax.numpy as jnp
from jax import lax

STEPS = 4
NX = 128
NY = 256
NZ = 1024


def steps_of(key, shape, shards, smallest, high):
    loudness = 1.0
    for position, shards_of in shards:
        steps = jax.random.uniform(jax.random.fold_in(jax.random.fold_in(key, 6), position), (shards_of,), jnp.float32, smallest / len(shards), high / len(shards))
        loudness = loudness * jnp.repeat(jnp.exp(steps), shape[position] // shards_of).reshape((-1,) + (1,) * (len(shape) - 1 - position))
    return loudness


def normal_values(stream_key, extent, scale, limit, pieces=(), held_as=jnp.bfloat16):
    loudness = steps_of(stream_key, extent, pieces, -0.22, 0.18) if pieces else 1.0
    drawn = jax.random.normal(stream_key, extent, jnp.float32) * scale * loudness
    return jnp.minimum(jnp.maximum(drawn, -limit), limit).astype(held_as)


def setup_inputs(seed: int = 0) -> dict:
    key_list = jax.random.split(jax.random.key(seed), 4)
    source = normal_values(key_list[0], (STEPS, NX, NY, NZ), 1.0, 6.0, ((2, 32), (3, 8)))
    speed = jnp.clip(jnp.exp(math.log(2.5) - 0.916290732 * jax.random.uniform(key_list[1], (NX, NY, NZ), jnp.float32) ** steps_of(key_list[1], (NX, NY, NZ), ((0, 32), (2, 8)), -0.2, 0.2)), 1.0, 2.5).astype(jnp.bfloat16)
    impedance = jnp.clip(jnp.exp(math.log(2.0) - 1.3862944 * jax.random.uniform(key_list[2], (NX, NY, NZ), jnp.float32) ** steps_of(key_list[2], (NX, NY, NZ), ((0, 32), (2, 8)), -0.2, 0.2)), 0.5, 2.0).astype(jnp.bfloat16)
    return dict(source=source, speed=speed, impedance=impedance)


courant = 0.15


def forward_diff(field, dim):
    widths = [(0, 0)] * field.ndim
    widths[dim] = (0, 1)
    padded = jnp.pad(field, widths)
    return lax.slice_in_dim(padded, 1, field.shape[dim] + 1, axis=dim) - field


def backward_diff(field, dim):
    widths = [(0, 0)] * field.ndim
    widths[dim] = (1, 0)
    padded = jnp.pad(field, widths)
    return field - lax.slice_in_dim(padded, 0, field.shape[dim], axis=dim)


def reference(source, speed, impedance):
    sound = speed.astype(jnp.float32)
    imped = impedance.astype(jnp.float32)
    stiff = sound * imped
    buoy = sound / imped
    pressure = jnp.zeros(speed.shape, jnp.float32)
    velocity = [jnp.zeros(speed.shape, jnp.float32) for _ in range(3)]
    for step in range(STEPS):
        pressure = pressure + source[STEPS - 1 - step].astype(jnp.float32)
        loaded = stiff * pressure
        velocity = [velocity[d] + courant * forward_diff(loaded, d) for d in range(3)]
        spread = backward_diff(buoy * velocity[0], 0) + backward_diff(buoy * velocity[1], 1)
        spread = spread + backward_diff(buoy * velocity[2], 2)
        pressure = pressure + courant * spread
    return pressure, jnp.stack(velocity)
```

```python
import jax
import jax.numpy as jnp
from jax import lax
from jax.experimental import pallas as pl
from jax.experimental.pallas import tpu as pltpu
from jax.sharding import PartitionSpec as P

courant = 0.15
MESH = pl.DeviceIdType.MESH
SLABS = 32
F32 = jnp.float32
BF16 = jnp.bfloat16


def slab_device(slab, gy):
    return (slab // 16, lax.rem(slab, 16), gy)


def rounded(x):
    return x.astype(BF16).astype(F32)


def packed(layer_of):
    row = lax.broadcasted_iota(jnp.int32, (16, 128), 0)
    lane = lax.broadcasted_iota(jnp.int32, (16, 128), 1)

    def add(j, total):
        pick = ((row == j) & (lane == 0)) | ((row == 8 + j) & (lane == 127))
        return total + lax.dot_general(
            jnp.where(pick, 1.0, 0.0).astype(BF16),
            layer_of(j),
            (((1,), (1,)), ((), ())),
            preferred_element_type=F32,
        )

    return lax.fori_loop(0, 8, add, jnp.zeros((16, 128), F32))


def kernel(src, speed, imp, pres, vel, acc, hs, sx, hx, zc, hc, zs, hz, stiff, buoy, p, vx, fx, load, fy, edge, vzm,
           send, recv, own_sem, cs_send, cs_recv, cz_send, cz_recv, x_send, x_recv, z_send, z_recv):
    gy = lax.axis_index("gy")
    s = lax.axis_index("grp") * 16 + lax.axis_index("gx")
    above, below = lax.rem(s + 1, SLABS), lax.rem(s + SLABS - 1, SLABS)
    z_above, z_below = lax.rem(gy + 1, 8), lax.rem(gy + 7, 8)
    x_to = (slab_device(above, gy), slab_device(below, gy))
    z_to = (slab_device(s, z_above), slab_device(s, z_below))

    barrier = pltpu.get_barrier_semaphore()

    def greet(d, _):
        pl.semaphore_signal(barrier, inc=1, device_id=slab_device(lax.rem(s + d, SLABS), gy), device_id_type=MESH)
        return 0

    lax.fori_loop(1, SLABS, greet, 0)
    for to in z_to:
        pl.semaphore_signal(barrier, inc=1, device_id=to, device_id_type=MESH)

    own = pltpu.make_async_copy(src.at[:, pl.ds(32 * s, 32)], acc.at[:, pl.ds(32 * s, 32)], own_sem)
    own.start()

    def coefficients(l, _):
        a, b = speed[l].astype(F32), imp[l].astype(F32)
        stiff[l + 1] = a * b
        buoy[l + 1] = a / b
        vel[0, l] = jnp.zeros((256, 128), F32)
        vel[1, l] = jnp.zeros((256, 128), F32)
        vel[2, l] = jnp.zeros((256, 128), F32)
        load[l + 1, 256:264] = jnp.zeros((8, 128), F32)
        return 0

    lax.fori_loop(0, 4, coefficients, 0)

    def zero_vx(l, _):
        vx[l] = jnp.zeros((256, 128), F32)
        return 0

    lax.fori_loop(0, 5, zero_vx, 0)
    fy[0:8] = jnp.zeros((8, 128), F32)
    vzm[...] = jnp.zeros((8, 128), F32)

    def half(ref, j):
        return ref[j // 2, pl.ds(pl.multiple_of(128 * lax.rem(j, 2), 128), 128)]

    packed_speed = packed(lambda j: half(speed, j))
    packed_imp = packed(lambda j: half(imp, j))
    zc[0, 0:8] = packed_speed[8:16]
    zc[0, 8:16] = packed_imp[8:16]
    zc[1, 0:8] = packed_speed[0:8]
    zc[1, 8:16] = packed_imp[0:8]

    pl.semaphore_wait(barrier, SLABS - 1 + 2)

    def exchange(n):
        def one(d, _):
            to = lax.rem(s + d, SLABS)
            pltpu.make_async_remote_copy(
                src.at[3 - n, pl.ds(32 * to, 32)], acc.at[3 - n, pl.ds(32 * s, 32)], send, recv.at[n],
                device_id=slab_device(to, gy), device_id_type=MESH).start()
            return 0

        lax.fori_loop(1, SLABS, one, 0)

    exchange(0)
    halo = []
    for way in range(2):
        layer = 3 - 3 * way
        for k, field in enumerate((speed, imp)):
            halo.append(pltpu.make_async_remote_copy(
                field.at[layer], hs.at[2 * way + k], cs_send.at[2 * way + k], cs_recv.at[2 * way + k],
                device_id=x_to[way], device_id_type=MESH))
        halo.append(pltpu.make_async_remote_copy(
            zc.at[way], hc.at[way], cz_send.at[way], cz_recv.at[way], device_id=z_to[way], device_id_type=MESH))
    for copy in halo:
        copy.start()
    for n in range(1, 4):
        exchange(n)
    own.wait()
    sent = []
    lane = lax.broadcasted_iota(jnp.int32, (256, 128), 1)
    has_below, has_above = jnp.where(s > 0, 1.0, 0.0), jnp.where(s < SLABS - 1, 1.0, 0.0)
    has_z_below, has_z_above = jnp.where(gy > 0, 1.0, 0.0), jnp.where(gy < 7, 1.0, 0.0)

    for n in range(4):
        pltpu.make_async_copy(acc.at[3 - n, 0:32 * 31], acc.at[3 - n, 0:32 * 31], recv.at[n]).wait()

        def add_source(b, _):
            x = acc[3 - n, pl.ds(pl.multiple_of(32 * b, 32), 32)].astype(F32).reshape(4, 8, 128)
            rows = pl.ds(pl.multiple_of(8 * b, 8), 8)
            p[1:5, rows] = x if n == 0 else p[1:5, rows] + x
            return 0

        lax.fori_loop(0, SLABS, add_source, 0)
        sx[n, 0] = p[4].astype(BF16)
        sx[n, 1] = p[1].astype(BF16)
        columns = packed(lambda j: half(p.at[1:5], j).astype(BF16))
        zs[n, 0] = columns[8:16]
        zs[n, 1] = columns[0:8]
        copies = []
        for way in range(2):
            copies.append(pltpu.make_async_remote_copy(
                sx.at[n, way], hx.at[n, way], x_send.at[n, way], x_recv.at[n, way],
                device_id=x_to[way], device_id_type=MESH))
            copies.append(pltpu.make_async_remote_copy(
                zs.at[n, way], hz.at[n, way], z_send.at[n, way], z_recv.at[n, way],
                device_id=z_to[way], device_id_type=MESH))
        for copy in copies:
            copy.start()
        if n == 0:
            for copy in halo:
                copy.wait_recv()
            stiff[0] = hs[0].astype(F32) * hs[1].astype(F32)
            buoy[0] = hs[0].astype(F32) / hs[1].astype(F32) * has_below
            stiff[5] = hs[2].astype(F32) * hs[3].astype(F32) * has_above
        for copy in copies:
            copy.wait_recv()
        sent += copies
        p[0] = hx[n, 0].astype(F32)
        p[5] = hx[n, 1].astype(F32)

        past = hc[1, 0:8] * hc[1, 8:16] * hz[n, 1] * has_z_above
        vzm[...] += courant * (zc[1, 0:8] * zc[1, 8:16] * zs[n, 1] - hc[0, 0:8] * hc[0, 8:16] * hz[n, 0])
        before = hc[0, 0:8] / hc[0, 8:16] * vzm[...] * has_z_below
        rows = jnp.concatenate(
            [rounded(past), past - rounded(past), rounded(before), before - rounded(before)], 0)
        columns = jnp.transpose(rows).astype(BF16)
        row32 = lax.broadcasted_iota(jnp.int32, (32, 128), 0)
        lane32 = lax.broadcasted_iota(jnp.int32, (32, 128), 1)

        def spread_edge(j, _):
            pick = (((row32 == j) | (row32 == 8 + j)) & (lane32 == 127)) | (
                ((row32 == 16 + j) | (row32 == 24 + j)) & (lane32 == 0))
            edge[j // 2, pl.ds(pl.multiple_of(128 * lax.rem(j, 2), 128), 128)] = jnp.dot(
                columns, jnp.where(pick, 1.0, 0.0).astype(BF16), preferred_element_type=F32)
            return 0

        lax.fori_loop(0, 8, spread_edge, 0)

        def loads(l, _):
            load[l, 0:256] = stiff[l] * p[l]
            return 0

        lax.fori_loop(0, 6, loads, 0)

        def x_part(l, _):
            v = vx[l] + courant * (load[l + 1, 0:256] - load[l, 0:256])
            vx[l] = v
            fx[l] = buoy[l] * v
            return 0

        lax.fori_loop(0, 5, x_part, 0)

        def layer(l, _):
            b = buoy[l + 1]
            here = load[l + 1, 0:256]
            v1 = vel[1, l] + courant * (load[l + 1, 1:257] - here)
            vel[1, l] = v1
            flux = b * v1
            fy[8:264] = flux
            total = (fx[l + 1] - fx[l]) + (flux - fy[7:263])
            rim = edge[l]
            v2 = vel[2, l] + courant * (jnp.where(lane == 127, rim, pltpu.roll(here, 127, 1)) - here)
            vel[2, l] = v2
            flux = b * v2
            total = total + (flux - jnp.where(lane == 0, rim, pltpu.roll(flux, 1, 1)))
            out = p[l + 1] + courant * total
            if n < 3:
                p[l + 1] = out
            else:
                pres[l] = out
                vel[0, l] = vx[l + 1]
            return 0

        lax.fori_loop(0, 4, layer, 0)

    for copy in halo + sent:
        copy.wait_send()
    pltpu.make_async_copy(acc.at[:, 0:32 * 31], acc.at[:, 0:32 * 31], send).wait()


def on_device(source, speed, impedance):
    vmem = pl.BlockSpec(memory_space=pltpu.VMEM)
    dma = pltpu.SemaphoreType.DMA
    return pl.pallas_call(
        kernel,
        out_shape=(
            jax.ShapeDtypeStruct((4, 256, 128), F32),
            jax.ShapeDtypeStruct((3, 4, 256, 128), F32),
        ),
        in_specs=[pl.BlockSpec(memory_space=pl.ANY), vmem, vmem],
        out_specs=(vmem, vmem),
        scratch_shapes=[
            pltpu.VMEM((4, 1024, 128), BF16),
            pltpu.VMEM((4, 256, 128), BF16),
            pltpu.VMEM((4, 2, 256, 128), BF16),
            pltpu.VMEM((4, 2, 256, 128), BF16),
            pltpu.VMEM((2, 16, 128), F32),
            pltpu.VMEM((2, 16, 128), F32),
            pltpu.VMEM((4, 2, 8, 128), F32),
            pltpu.VMEM((4, 2, 8, 128), F32),
            pltpu.VMEM((6, 256, 128), F32),
            pltpu.VMEM((5, 256, 128), F32),
            pltpu.VMEM((6, 256, 128), F32),
            pltpu.VMEM((5, 256, 128), F32),
            pltpu.VMEM((5, 256, 128), F32),
            pltpu.VMEM((6, 264, 128), F32),
            pltpu.VMEM((264, 128), F32),
            pltpu.VMEM((4, 256, 128), F32),
            pltpu.VMEM((8, 128), F32),
            dma, dma((4,)), dma, dma((4,)), dma((4,)), dma((2,)), dma((2,)),
            dma((4, 2)), dma((4, 2)), dma((4, 2)), dma((4, 2)),
        ],
        compiler_params=pltpu.CompilerParams(
            collective_id=0, has_side_effects=True, vmem_limit_bytes=48 * 1024 * 1024),
    )(source.reshape(4, 1024, 128), speed, impedance)


def solution(mesh):
    in_specs = (
        P(None, None, ("grp", "gx"), "gy"),
        P(("grp", "gx"), None, "gy"),
        P(("grp", "gx"), None, "gy"),
    )
    out_specs = (P(("grp", "gx"), None, "gy"), P(None, ("grp", "gx"), None, "gy"))
    return jax.shard_map(on_device, mesh=mesh, in_specs=in_specs, out_specs=out_specs, check_vma=False)
```

```python
import jax
import jax.numpy as jnp
from jax import lax
from jax.experimental import pallas as pl
from jax.experimental.pallas import tpu as pltpu
from jax.sharding import PartitionSpec as P

courant = 0.15
MESH = pl.DeviceIdType.MESH
SLABS = 32
F32 = jnp.float32
BF16 = jnp.bfloat16
PLAN = {'start': ((1, 1, 32),), 'sent0': ((2, 1, 32),), 'sent1': ((3, 1, 32),)}


def slab_device(slab, gy):
    return (slab // 16, lax.rem(slab, 16), gy)


def rounded(x):
    return x.astype(BF16).astype(F32)


def packed(layer_of):
    row = lax.broadcasted_iota(jnp.int32, (16, 128), 0)
    lane = lax.broadcasted_iota(jnp.int32, (16, 128), 1)
    total = None
    for j in range(8):
        pick = ((row == j) & (lane == 0)) | ((row == 8 + j) & (lane == 127))
        part = lax.dot_general(
            jnp.where(pick, 1.0, 0.0).astype(BF16),
            layer_of(j),
            (((1,), (1,)), ((), ())),
            preferred_element_type=F32,
        )
        total = part if total is None else total + part
    return total


def kernel(src, speed, imp, pres, vel, acc, sp, im, hs, sx, hx, zc, hc, zs, hz, stiff, buoy, vxm, fx, load, fy,
           total, edge, vzm, send, recv, own_sem, cs_send, cs_recv, cz_send, cz_recv, x_send, x_recv, z_send, z_recv):
    gy = lax.axis_index("gy")
    s = lax.axis_index("grp") * 16 + lax.axis_index("gx")
    above, below = lax.rem(s + 1, SLABS), lax.rem(s + SLABS - 1, SLABS)
    z_above, z_below = lax.rem(gy + 1, 8), lax.rem(gy + 7, 8)
    x_to = (slab_device(above, gy), slab_device(below, gy))
    z_to = (slab_device(s, z_above), slab_device(s, z_below))

    barrier = pltpu.get_barrier_semaphore()

    def greet(d, _):
        pl.semaphore_signal(barrier, inc=1, device_id=slab_device(lax.rem(s + d, SLABS), gy), device_id_type=MESH)
        return 0

    lax.fori_loop(1, SLABS, greet, 0)
    for to in z_to:
        pl.semaphore_signal(barrier, inc=1, device_id=to, device_id_type=MESH)

    own = pltpu.make_async_copy(src.at[:, pl.ds(32 * s, 32)], acc.at[:, pl.ds(32 * s, 32)], own_sem.at[0])
    own.start()
    fetch = (pltpu.make_async_copy(speed, sp, own_sem.at[1]), pltpu.make_async_copy(imp, im, own_sem.at[2]))
    for copy in fetch:
        copy.start()
    zero = jnp.zeros((256, 128), F32)

    def clear(l, _):
        for d in range(3):
            vel[d, l] = zero
        load[l, 256:264] = jnp.zeros((8, 128), F32)
        return 0

    lax.fori_loop(0, 4, clear, 0)
    vxm[...] = zero
    fy[0:8] = jnp.zeros((8, 128), F32)
    vzm[...] = jnp.zeros((8, 128), F32)
    for copy in fetch:
        copy.wait()

    def coefficients(l, _):
        a, b = sp[l].astype(F32), im[l].astype(F32)
        stiff[l + 1] = a * b
        buoy[l + 1] = a / b
        return 0

    lax.fori_loop(0, 4, coefficients, 0)

    packed_speed = packed(lambda j: sp[j // 2, 128 * (j % 2):128 * (j % 2) + 128])
    packed_imp = packed(lambda j: im[j // 2, 128 * (j % 2):128 * (j % 2) + 128])
    zc[0, 0:8] = packed_speed[8:16]
    zc[0, 8:16] = packed_imp[8:16]
    zc[1, 0:8] = packed_speed[0:8]
    zc[1, 8:16] = packed_imp[0:8]

    pl.semaphore_wait(barrier, SLABS - 1 + 2)

    def exchange(n, first, end):
        def one(d, _):
            to = lax.rem(s + d, SLABS)
            pltpu.make_async_remote_copy(
                src.at[3 - n, pl.ds(32 * to, 32)], acc.at[3 - n, pl.ds(32 * s, 32)], send, recv.at[n],
                device_id=slab_device(to, gy), device_id_type=MESH).start()
            return 0

        lax.fori_loop(first, end, one, 0)

    def exchanges(place):
        for part in PLAN.get(place, ()):
            exchange(*part)

    exchange(0, 1, SLABS)
    halo_x, halo_z = [], []
    for way in range(2):
        layer = 3 - 3 * way
        for k, field in enumerate((sp, im)):
            halo_x.append(pltpu.make_async_remote_copy(
                field.at[layer], hs.at[2 * way + k], cs_send.at[2 * way + k], cs_recv.at[2 * way + k],
                device_id=x_to[way], device_id_type=MESH))
        halo_z.append(pltpu.make_async_remote_copy(
            zc.at[way], hc.at[way], cz_send.at[way], cz_recv.at[way], device_id=z_to[way], device_id_type=MESH))
    for copy in halo_z + halo_x:
        copy.start()
    exchanges("start")
    own.wait()
    sent = halo_x + halo_z
    lane = lax.broadcasted_iota(jnp.int32, (256, 128), 1)
    has_below, has_above = jnp.where(s > 0, 1.0, 0.0), jnp.where(s < SLABS - 1, 1.0, 0.0)
    has_z_below, has_z_above = jnp.where(gy > 0, 1.0, 0.0), jnp.where(gy < 7, 1.0, 0.0)

    for n in range(4):
        pltpu.make_async_copy(acc.at[3 - n, 0:32 * 31], acc.at[3 - n, 0:32 * 31], recv.at[n]).wait()

        def add_source(i, _):
            x = acc[3 - n, pl.ds(pl.multiple_of(64 * i, 64), 64)].astype(F32).reshape(2, 4, 8, 128)
            rows = pl.ds(pl.multiple_of(16 * i, 16), 16)
            for l in range(4):
                now = x[:, l].reshape(16, 128)
                if n > 0:
                    now = pres[l, rows] + now
                pres[l, rows] = now
                if l in (0, 3):
                    sx[n, 0 if l == 3 else 1, rows] = now.astype(BF16)
            return 0

        lax.fori_loop(0, 16, add_source, 0, unroll=4)
        copies_x, copies_z = [], []
        for way in range(2):
            copies_x.append(pltpu.make_async_remote_copy(
                sx.at[n, way], hx.at[n, way], x_send.at[n, way], x_recv.at[n, way],
                device_id=x_to[way], device_id_type=MESH))
            copies_z.append(pltpu.make_async_remote_copy(
                zs.at[n, way], hz.at[n, way], z_send.at[n, way], z_recv.at[n, way],
                device_id=z_to[way], device_id_type=MESH))
        sent += copies_x + copies_z
        for copy in copies_x:
            copy.start()
        columns = packed(lambda j: pres[j // 2, 128 * (j % 2):128 * (j % 2) + 128].astype(BF16))
        zs[n, 0] = columns[8:16]
        zs[n, 1] = columns[0:8]
        for copy in copies_z:
            copy.start()
        exchanges(f"sent{n}")

        def inner(l, _):
            here = stiff[l + 1] * pres[l]
            load[l, 0:256] = here
            v1 = vel[1, l] + courant * (load[l, 1:257] - here)
            vel[1, l] = v1
            flux = buoy[l + 1] * v1
            fy[8:264] = flux
            total[l] = flux - fy[7:263]
            vel[2, l] = vel[2, l] + courant * (jnp.where(lane == 127, 0.0, pltpu.roll(here, 127, 1)) - here)
            return 0

        lax.fori_loop(0, 4, inner, 0)

        def inner_x(l, _):
            v = vel[0, l] + courant * (load[l + 1, 0:256] - load[l, 0:256])
            vel[0, l] = v
            flux = buoy[l + 1] * v
            fx[l] = flux
            return 0

        lax.fori_loop(0, 3, inner_x, 0)
        exchanges(f"inner{n}")

        if n == 0:
            for copy in halo_z:
                copy.wait_recv()
        for copy in copies_z:
            copy.wait_recv()
        past = hc[1, 0:8] * hc[1, 8:16] * hz[n, 1] * has_z_above
        before_v = vzm[...] + courant * (zc[1, 0:8] * zc[1, 8:16] * zs[n, 1] - hc[0, 0:8] * hc[0, 8:16] * hz[n, 0])
        vzm[...] = before_v
        before = hc[0, 0:8] / hc[0, 8:16] * before_v * has_z_below
        rows = jnp.concatenate(
            [rounded(past), past - rounded(past), rounded(before), before - rounded(before)], 0)
        columns = jnp.transpose(rows).astype(BF16)
        row32 = lax.broadcasted_iota(jnp.int32, (32, 128), 0)
        lane32 = lax.broadcasted_iota(jnp.int32, (32, 128), 1)
        for j in range(8):
            pick = (((row32 == j) | (row32 == 8 + j)) & (lane32 == 127)) | (
                ((row32 == 16 + j) | (row32 == 24 + j)) & (lane32 == 0))
            edge[j // 2, 128 * (j % 2):128 * (j % 2) + 128] = jnp.dot(
                columns, jnp.where(pick, 1.0, 0.0).astype(BF16), preferred_element_type=F32)

        def outer_z(l, _):
            rim = edge[l]
            v2 = vel[2, l] + courant * jnp.where(lane == 127, rim, 0.0)
            vel[2, l] = v2
            flux = buoy[l + 1] * v2
            total[l] = total[l] + (flux - jnp.where(lane == 0, rim, pltpu.roll(flux, 1, 1)))
            return 0

        lax.fori_loop(0, 4, outer_z, 0)

        def middle(l, _):
            pres[l] = pres[l] + courant * (total[l] + (fx[l] - fx[l - 1]))
            return 0

        lax.fori_loop(1, 3, middle, 0)
        exchanges(f"third{n}")

        if n == 0:
            for copy in halo_x:
                copy.wait_recv()
            stiff[0] = hs[0].astype(F32) * hs[1].astype(F32)
            buoy[0] = hs[0].astype(F32) / hs[1].astype(F32) * has_below
            stiff[5] = hs[2].astype(F32) * hs[3].astype(F32) * has_above
        for copy in copies_x:
            copy.wait_recv()
        v = vxm[...] + courant * (load[0, 0:256] - stiff[0] * hx[n, 0].astype(F32))
        vxm[...] = v
        pres[0] = pres[0] + courant * (total[0] + (fx[0] - buoy[0] * v))
        v = vel[0, 3] + courant * (stiff[5] * hx[n, 1].astype(F32) - load[3, 0:256])
        vel[0, 3] = v
        pres[3] = pres[3] + courant * (total[3] + (buoy[4] * v - fx[2]))

    for copy in sent:
        copy.wait_send()
    pltpu.make_async_copy(acc.at[:, 0:32 * 31], acc.at[:, 0:32 * 31], send).wait()


def on_device(source, speed, impedance):
    vmem = pl.BlockSpec(memory_space=pltpu.VMEM)
    hbm = pl.BlockSpec(memory_space=pltpu.HBM)
    dma = pltpu.SemaphoreType.DMA
    return pl.pallas_call(
        kernel,
        out_shape=(
            jax.ShapeDtypeStruct((4, 256, 128), F32),
            jax.ShapeDtypeStruct((3, 4, 256, 128), F32),
        ),
        in_specs=[hbm, hbm, hbm],
        out_specs=(vmem, vmem),
        scratch_shapes=[
            pltpu.VMEM((4, 1024, 128), BF16),
            pltpu.VMEM((4, 256, 128), BF16),
            pltpu.VMEM((4, 256, 128), BF16),
            pltpu.VMEM((4, 256, 128), BF16),
            pltpu.VMEM((4, 2, 256, 128), BF16),
            pltpu.VMEM((4, 2, 256, 128), BF16),
            pltpu.VMEM((2, 16, 128), F32),
            pltpu.VMEM((2, 16, 128), F32),
            pltpu.VMEM((4, 2, 8, 128), F32),
            pltpu.VMEM((4, 2, 8, 128), F32),
            pltpu.VMEM((6, 256, 128), F32),
            pltpu.VMEM((5, 256, 128), F32),
            pltpu.VMEM((256, 128), F32),
            pltpu.VMEM((3, 256, 128), F32),
            pltpu.VMEM((4, 264, 128), F32),
            pltpu.VMEM((264, 128), F32),
            pltpu.VMEM((4, 256, 128), F32),
            pltpu.VMEM((4, 256, 128), F32),
            pltpu.VMEM((8, 128), F32),
            dma, dma((4,)), dma((3,)), dma((4,)), dma((4,)), dma((2,)), dma((2,)),
            dma((4, 2)), dma((4, 2)), dma((4, 2)), dma((4, 2)),
        ],
        compiler_params=pltpu.CompilerParams(
            collective_id=0, has_side_effects=True, vmem_limit_bytes=48 * 1024 * 1024),
    )(source.reshape(4, 1024, 128), speed, impedance)


def solution(mesh):
    in_specs = (
        P(None, None, ("grp", "gx"), "gy"),
        P(("grp", "gx"), None, "gy"),
        P(("grp", "gx"), None, "gy"),
    )
    out_specs = (P(("grp", "gx"), None, "gy"), P(None, ("grp", "gx"), None, "gy"))
    return jax.shard_map(on_device, mesh=mesh, in_specs=in_specs, out_specs=out_specs, check_vma=False)
```

```python
import jax
import jax.numpy as jnp
from jax import lax
from jax.experimental import pallas as pl
from jax.experimental.pallas import tpu as pltpu
from jax.sharding import PartitionSpec as P

courant = 0.15
MESH = pl.DeviceIdType.MESH
SLABS = 32
F32 = jnp.float32
BF16 = jnp.bfloat16
STRIDE = 1
PLAN = {'start': ((1, 1, 32),), 'sent0': ((2, 1, 32),), 'sent1': ((3, 1, 32),)}


def slab_device(slab, gy):
    return (slab // 16, lax.rem(slab, 16), gy)


def rounded(x):
    return x.astype(BF16).astype(F32)


def packed(layer_of):
    row = lax.broadcasted_iota(jnp.int32, (16, 128), 0)
    lane = lax.broadcasted_iota(jnp.int32, (16, 128), 1)
    total = None
    for j in range(8):
        pick = ((row == j) & (lane == 0)) | ((row == 8 + j) & (lane == 127))
        part = lax.dot_general(
            jnp.where(pick, 1.0, 0.0).astype(BF16),
            layer_of(j),
            (((1,), (1,)), ((), ())),
            preferred_element_type=F32,
        )
        total = part if total is None else total + part
    return total


def kernel(src, speed, imp, pres, vel, acc, sp, im, hs, sx, hx, zc, hc, zs, hz, stiff, buoy, vxm, fx, load, fy,
           total, edge, vzm, send, recv, own_sem, cs_send, cs_recv, cz_send, cz_recv, x_send, x_recv, z_send, z_recv):
    gy = lax.axis_index("gy")
    s = lax.axis_index("grp") * 16 + lax.axis_index("gx")
    above, below = lax.rem(s + 1, SLABS), lax.rem(s + SLABS - 1, SLABS)
    z_above, z_below = lax.rem(gy + 1, 8), lax.rem(gy + 7, 8)
    x_to = (slab_device(above, gy), slab_device(below, gy))
    z_to = (slab_device(s, z_above), slab_device(s, z_below))

    barrier = pltpu.get_barrier_semaphore()

    def greet(d, _):
        pl.semaphore_signal(barrier, inc=1, device_id=slab_device(lax.rem(s + d, SLABS), gy), device_id_type=MESH)
        return 0

    lax.fori_loop(1, SLABS, greet, 0)
    for to in z_to:
        pl.semaphore_signal(barrier, inc=1, device_id=to, device_id_type=MESH)

    own = pltpu.make_async_copy(src.at[:, pl.ds(32 * s, 32)], acc.at[:, pl.ds(32 * s, 32)], own_sem.at[0])
    own.start()
    fetch = (pltpu.make_async_copy(speed, sp, own_sem.at[1]), pltpu.make_async_copy(imp, im, own_sem.at[2]))
    for copy in fetch:
        copy.start()
    zero = jnp.zeros((256, 128), F32)

    def clear(l, _):
        for d in range(3):
            vel[d, l] = zero
        load[l, 256:264] = jnp.zeros((8, 128), F32)
        return 0

    lax.fori_loop(0, 4, clear, 0)
    vxm[...] = zero
    fy[0:8] = jnp.zeros((8, 128), F32)
    vzm[...] = jnp.zeros((8, 128), F32)
    for copy in fetch:
        copy.wait()

    def coefficients(l, _):
        a, b = sp[l].astype(F32), im[l].astype(F32)
        stiff[l] = a * b
        buoy[l + 1] = a / b
        return 0

    lax.fori_loop(0, 4, coefficients, 0)
    hs[0] = buoy[4].astype(BF16)

    packed_speed = packed(lambda j: sp[j // 2, 128 * (j % 2):128 * (j % 2) + 128])
    packed_imp = packed(lambda j: im[j // 2, 128 * (j % 2):128 * (j % 2) + 128])
    zc[0:8] = packed_speed[8:16]
    zc[8:16] = packed_imp[8:16]

    pl.semaphore_wait(barrier, SLABS - 1 + 2)

    def exchange(n, first, end):
        def one(d, _):
            to = lax.rem(s + 1 + lax.rem((d - 1) * STRIDE, SLABS - 1), SLABS)
            pltpu.make_async_remote_copy(
                src.at[3 - n, pl.ds(32 * to, 32)], acc.at[3 - n, pl.ds(32 * s, 32)], send, recv.at[n],
                device_id=slab_device(to, gy), device_id_type=MESH).start()
            return 0

        lax.fori_loop(first, end, one, 0)

    def exchanges(place):
        for part in PLAN.get(place, ()):
            exchange(*part)

    exchange(0, 1, SLABS)
    halo_x, halo_z = [], []
    halo_z.append(pltpu.make_async_remote_copy(zc, hc, cz_send, cz_recv, device_id=z_to[0], device_id_type=MESH))
    halo_x.append(pltpu.make_async_remote_copy(
        hs.at[0], hs.at[1], cs_send, cs_recv, device_id=x_to[0], device_id_type=MESH))
    for copy in halo_z:
        copy.start()
    exchanges("start")
    for copy in halo_x:
        copy.start()
    own.wait()
    sent = halo_x + halo_z
    lane = lax.broadcasted_iota(jnp.int32, (256, 128), 1)
    has_below, has_above = jnp.where(s > 0, 1.0, 0.0), jnp.where(s < SLABS - 1, 1.0, 0.0)
    has_z_below, has_z_above = jnp.where(gy > 0, 1.0, 0.0), jnp.where(gy < 7, 1.0, 0.0)

    for n in range(4):
        pltpu.make_async_copy(acc.at[3 - n, 0:32 * 31], acc.at[3 - n, 0:32 * 31], recv.at[n]).wait()

        def add_source(i, _):
            x = acc[3 - n, pl.ds(pl.multiple_of(64 * i, 64), 64)].astype(F32).reshape(2, 4, 8, 128)
            rows = pl.ds(pl.multiple_of(16 * i, 16), 16)
            for l in range(4):
                now = x[:, l].reshape(16, 128)
                if n > 0:
                    now = pres[l, rows] + now
                pres[l, rows] = now
                now = stiff[l, rows] * now
                load[l, rows] = now
                if l in (0, 3):
                    sx[n, 0 if l == 3 else 1, rows] = now.astype(BF16)
            return 0

        lax.fori_loop(0, 16, add_source, 0, unroll=4)
        copies_x, copies_z = [], []
        for way in range(2):
            copies_x.append(pltpu.make_async_remote_copy(
                sx.at[n, way], hx.at[n, way], x_send.at[n, way], x_recv.at[n, way],
                device_id=x_to[way], device_id_type=MESH))
            copies_z.append(pltpu.make_async_remote_copy(
                zs.at[n, way], hz.at[n, way], z_send.at[n, way], z_recv.at[n, way],
                device_id=z_to[way], device_id_type=MESH))
        sent += copies_x + copies_z
        columns = packed(lambda j: load[j // 2, 128 * (j % 2):128 * (j % 2) + 128].astype(BF16))
        zs[n, 0] = columns[8:16]
        zs[n, 1] = columns[0:8]
        for copy in copies_z + copies_x:
            copy.start()
        exchanges(f"sent{n}")

        def inner(l, _):
            here = load[l, 0:256]
            v1 = vel[1, l] + courant * (load[l, 1:257] - here)
            vel[1, l] = v1
            flux = buoy[l + 1] * v1
            fy[8:264] = flux
            total[l] = flux - fy[7:263]
            vel[2, l] = vel[2, l] + courant * (jnp.where(lane == 127, 0.0, pltpu.roll(here, 127, 1)) - here)
            return 0

        lax.fori_loop(0, 4, inner, 0)

        def inner_x(l, _):
            v = vel[0, l] + courant * (load[l + 1, 0:256] - load[l, 0:256])
            vel[0, l] = v
            flux = buoy[l + 1] * v
            fx[l] = flux
            return 0

        lax.fori_loop(0, 3, inner_x, 0)
        exchanges(f"inner{n}")

        if n == 0:
            for copy in halo_z:
                copy.wait_recv()
        for copy in copies_z:
            copy.wait_recv()
        past = hz[n, 1] * has_z_above
        before_v = vzm[...] + courant * (zs[n, 1] - hz[n, 0])
        vzm[...] = before_v
        before = hc[0:8] / hc[8:16] * before_v * has_z_below
        rows = jnp.concatenate(
            [rounded(past), past - rounded(past), rounded(before), before - rounded(before)], 0)
        columns = jnp.transpose(rows).astype(BF16)
        row32 = lax.broadcasted_iota(jnp.int32, (32, 128), 0)
        lane32 = lax.broadcasted_iota(jnp.int32, (32, 128), 1)
        for j in range(8):
            pick = (((row32 == j) | (row32 == 8 + j)) & (lane32 == 127)) | (
                ((row32 == 16 + j) | (row32 == 24 + j)) & (lane32 == 0))
            edge[j // 2, 128 * (j % 2):128 * (j % 2) + 128] = jnp.dot(
                columns, jnp.where(pick, 1.0, 0.0).astype(BF16), preferred_element_type=F32)

        def outer_z(l, _):
            rim = edge[l]
            v2 = vel[2, l] + courant * jnp.where(lane == 127, rim, 0.0)
            vel[2, l] = v2
            flux = buoy[l + 1] * v2
            total[l] = total[l] + (flux - jnp.where(lane == 0, rim, pltpu.roll(flux, 1, 1)))
            return 0

        lax.fori_loop(0, 4, outer_z, 0)

        def middle(l, _):
            pres[l] = pres[l] + courant * (total[l] + (fx[l] - fx[l - 1]))
            return 0

        lax.fori_loop(1, 3, middle, 0)
        exchanges(f"third{n}")

        if n == 0:
            for copy in halo_x:
                copy.wait_recv()
            buoy[0] = hs[1].astype(F32) * has_below
        for copy in copies_x:
            copy.wait_recv()
        v = vxm[...] + courant * (load[0, 0:256] - hx[n, 0].astype(F32))
        vxm[...] = v
        pres[0] = pres[0] + courant * (total[0] + (fx[0] - buoy[0] * v))
        v = vel[0, 3] + courant * (hx[n, 1].astype(F32) * has_above - load[3, 0:256])
        vel[0, 3] = v
        pres[3] = pres[3] + courant * (total[3] + (buoy[4] * v - fx[2]))

    for copy in sent:
        copy.wait_send()
    pltpu.make_async_copy(acc.at[:, 0:32 * 31], acc.at[:, 0:32 * 31], send).wait()


def on_device(source, speed, impedance):
    vmem = pl.BlockSpec(memory_space=pltpu.VMEM)
    hbm = pl.BlockSpec(memory_space=pltpu.HBM)
    dma = pltpu.SemaphoreType.DMA
    return pl.pallas_call(
        kernel,
        out_shape=(
            jax.ShapeDtypeStruct((4, 256, 128), F32),
            jax.ShapeDtypeStruct((3, 4, 256, 128), F32),
        ),
        in_specs=[hbm, hbm, hbm],
        out_specs=(vmem, vmem),
        scratch_shapes=[
            pltpu.VMEM((4, 1024, 128), BF16),
            pltpu.VMEM((4, 256, 128), BF16),
            pltpu.VMEM((4, 256, 128), BF16),
            pltpu.VMEM((2, 256, 128), BF16),
            pltpu.VMEM((4, 2, 256, 128), BF16),
            pltpu.VMEM((4, 2, 256, 128), BF16),
            pltpu.VMEM((16, 128), F32),
            pltpu.VMEM((16, 128), F32),
            pltpu.VMEM((4, 2, 8, 128), F32),
            pltpu.VMEM((4, 2, 8, 128), F32),
            pltpu.VMEM((4, 256, 128), F32),
            pltpu.VMEM((5, 256, 128), F32),
            pltpu.VMEM((256, 128), F32),
            pltpu.VMEM((3, 256, 128), F32),
            pltpu.VMEM((4, 264, 128), F32),
            pltpu.VMEM((264, 128), F32),
            pltpu.VMEM((4, 256, 128), F32),
            pltpu.VMEM((4, 256, 128), F32),
            pltpu.VMEM((8, 128), F32),
            dma, dma((4,)), dma((3,)), dma, dma, dma, dma,
            dma((4, 2)), dma((4, 2)), dma((4, 2)), dma((4, 2)),
        ],
        compiler_params=pltpu.CompilerParams(
            collective_id=0, has_side_effects=True, vmem_limit_bytes=48 * 1024 * 1024),
    )(*(pltpu.with_memory_space_constraint(a, pltpu.HBM) for a in (source.reshape(4, 1024, 128), speed, impedance)))


def solution(mesh):
    in_specs = (
        P(None, None, ("grp", "gx"), "gy"),
        P(("grp", "gx"), None, "gy"),
        P(("grp", "gx"), None, "gy"),
    )
    out_specs = (P(("grp", "gx"), None, "gy"), P(None, ("grp", "gx"), None, "gy"))
    return jax.shard_map(on_device, mesh=mesh, in_specs=in_specs, out_specs=out_specs, check_vma=False)
```

```python
import jax
import jax.numpy as jnp
from jax import lax
from jax.experimental import pallas as pl
from jax.experimental.pallas import tpu as pltpu
from jax.sharding import PartitionSpec as P

courant = 0.15
MESH = pl.DeviceIdType.MESH
SLABS = 32
F32 = jnp.float32
BF16 = jnp.bfloat16
STRIDE = 1
PLAN = {'half0': ((1, 1, 32),), 'sent0': ((2, 1, 32),), 'sent1': ((3, 1, 32),)}


def slab_device(slab, gy):
    return (slab // 16, lax.rem(slab, 16), gy)


def rounded(x):
    return x.astype(BF16).astype(F32)


def packed(layer_of, blocks=range(8)):
    row = lax.broadcasted_iota(jnp.int32, (16, 128), 0)
    lane = lax.broadcasted_iota(jnp.int32, (16, 128), 1)
    total = None
    for j in blocks:
        pick = ((row == j) & (lane == 0)) | ((row == 8 + j) & (lane == 127))
        part = lax.dot_general(
            jnp.where(pick, 1.0, 0.0).astype(BF16),
            layer_of(j),
            (((1,), (1,)), ((), ())),
            preferred_element_type=F32,
        )
        total = part if total is None else total + part
    return total


def kernel(src, speed, imp, pres, vel, acc, sp, im, hs, sx, hx, zc, hc, zs, hz, stiff, buoy, vxm, fx, load, fy,
           total, edge, vzm, owed, shares, zo, send, recv, own_sem, cs_send, cs_recv, cz_send, cz_recv, x_send, x_recv, z_send, z_recv):
    gy = lax.axis_index("gy")
    s = lax.axis_index("grp") * 16 + lax.axis_index("gx")
    above, below = lax.rem(s + 1, SLABS), lax.rem(s + SLABS - 1, SLABS)
    z_above, z_below = lax.rem(gy + 1, 8), lax.rem(gy + 7, 8)
    x_to = (slab_device(above, gy), slab_device(below, gy))
    z_to = (slab_device(s, z_above), slab_device(s, z_below))

    barrier = pltpu.get_barrier_semaphore()

    def greet(d, _):
        pl.semaphore_signal(barrier, inc=1, device_id=slab_device(lax.rem(s + d, SLABS), gy), device_id_type=MESH)
        return 0

    lax.fori_loop(1, SLABS, greet, 0)
    for to in z_to:
        pl.semaphore_signal(barrier, inc=1, device_id=to, device_id_type=MESH)

    own = pltpu.make_async_copy(src.at[:, pl.ds(32 * s, 32)], acc.at[:, pl.ds(32 * s, 32)], own_sem.at[0])
    own.start()
    fetch = (pltpu.make_async_copy(speed, sp, own_sem.at[1]), pltpu.make_async_copy(imp, im, own_sem.at[2]))
    for copy in fetch:
        copy.start()
    zero = jnp.zeros((256, 128), F32)

    def clear(l, _):
        for d in range(3):
            vel[d, l] = zero
        load[l, 256:264] = jnp.zeros((8, 128), F32)
        return 0

    lax.fori_loop(0, 4, clear, 0)
    vxm[...] = zero
    fy[0:8] = jnp.zeros((8, 128), F32)
    vzm[...] = jnp.zeros((8, 128), F32)
    for copy in fetch:
        copy.wait()

    def coefficients(l, _):
        a, b = sp[l].astype(F32), im[l].astype(F32)
        stiff[l] = a * b
        buoy[l + 1] = a / b
        return 0

    lax.fori_loop(0, 4, coefficients, 0)
    hs[0] = buoy[4].astype(BF16)

    packed_speed = packed(lambda j: sp[j // 2, 128 * (j % 2):128 * (j % 2) + 128])
    packed_imp = packed(lambda j: im[j // 2, 128 * (j % 2):128 * (j % 2) + 128])
    zo[0:16] = packed_speed
    zo[16:32] = packed_imp
    zc[0:8] = packed_speed[8:16]
    zc[8:16] = packed_imp[8:16]

    pl.semaphore_wait(barrier, SLABS - 1 + 2)

    def exchange_half(n, first, end, half):
        def one(d, _):
            to = lax.rem(s + 1 + lax.rem((d - 1) * STRIDE, SLABS - 1), SLABS)
            pltpu.make_async_remote_copy(
                src.at[3 - n, pl.ds(32 * to, 32)], acc.at[3 - n, pl.ds(32 * s, 32)], send, recv.at[n, half],
                device_id=slab_device(to, gy), device_id_type=MESH).start()
            return 0

        lax.fori_loop(first, end, one, 0)

    def exchange(n, first, end):
        if first < 16:
            exchange_half(n, first, min(end, 16), 0)
        if end > 16:
            exchange_half(n, max(first, 16), end, 1)

    def exchanges(place):
        for part in PLAN.get(place, ()):
            exchange(*part)

    halo_x = [pltpu.make_async_remote_copy(
        hs.at[0], hs.at[1], cs_send, cs_recv, device_id=x_to[0], device_id_type=MESH)]
    halo_z = [pltpu.make_async_remote_copy(zc, hc, cz_send, cz_recv, device_id=z_to[0], device_id_type=MESH)]
    for copy in halo_z + halo_x:
        copy.start()
    exchange(0, 1, SLABS)
    exchanges("start")
    own.wait()
    sent = halo_x + halo_z
    lane = lax.broadcasted_iota(jnp.int32, (256, 128), 1)
    has_below, has_above = jnp.where(s > 0, 1.0, 0.0), jnp.where(s < SLABS - 1, 1.0, 0.0)
    has_z_below, has_z_above = jnp.where(gy > 0, 1.0, 0.0), jnp.where(gy < 7, 1.0, 0.0)

    def add_source(n):
        for half in range(2):
            blocks = acc.at[3 - n, 0:32 * (15 + half)]
            pltpu.make_async_copy(blocks, blocks, recv.at[n, half]).wait()
            if half == 0:
                exchanges(f"half{n}")

        def one(i, _):
            x = acc[3 - n, pl.ds(pl.multiple_of(64 * i, 64), 64)].astype(F32).reshape(2, 4, 8, 128)
            rows = pl.ds(pl.multiple_of(16 * i, 16), 16)
            for l in range(4):
                now = x[:, l].reshape(16, 128)
                if n > 0:
                    now = pres[l, rows] + now
                pres[l, rows] = now
                now = stiff[l, rows] * now
                load[l, rows] = now
                if n == 0 and l in (0, 3):
                    sx[n, 0 if l == 3 else 1, rows] = now.astype(BF16)
            return 0

        lax.fori_loop(0, 16, one, 0, unroll=4)

    def send_halos(n, buffers, sems, to):
        copies = [
            pltpu.make_async_remote_copy(
                buffers[0].at[n, way], buffers[1].at[n, way], sems[0].at[n, way], sems[1].at[n, way],
                device_id=to[way], device_id_type=MESH)
            for way in range(2)]
        sent.extend(copies)
        for copy in copies:
            copy.start()
        return copies

    def load_part(j):
        return load[j // 2, 128 * (j % 2):128 * (j % 2) + 128].astype(BF16)

    def owed_part(j):
        return owed[j // 6, 128 * (j % 2):128 * (j % 2) + 128]

    row32 = lax.broadcasted_iota(jnp.int32, (32, 128), 0)
    lane32 = lax.broadcasted_iota(jnp.int32, (32, 128), 1)

    def spread(columns, j):
        pick = (((row32 == j) | (row32 == 8 + j)) & (lane32 == 127)) | (
            ((row32 == 16 + j) | (row32 == 24 + j)) & (lane32 == 0))
        edge[j // 2, 128 * (j % 2):128 * (j % 2) + 128] = jnp.dot(
            columns, jnp.where(pick, 1.0, 0.0).astype(BF16), preferred_element_type=F32)

    def rim_share(l):
        rim = edge[l]
        dv = courant * jnp.where(lane == 127, rim, 0.0)
        vel[2, l] = vel[2, l] + dv
        return courant * (buoy[l + 1] * dv - jnp.where(lane == 0, rim, 0.0))

    add_source(0)
    copies_x = send_halos(0, (sx, hx), (x_send, x_recv), x_to)
    columns = packed(load_part)
    zs[0, 0] = columns[8:16]
    zs[0, 1] = columns[0:8]
    copies_z = send_halos(0, (zs, hz), (z_send, z_recv), z_to)
    for n in range(4):
        exchanges(f"sent{n}")

        def inner(l, _):
            here = load[l, 0:256]
            v1 = vel[1, l] + courant * (load[l, 1:257] - here)
            vel[1, l] = v1
            flux = buoy[l + 1] * v1
            fy[8:264] = flux
            part = flux - fy[7:263]
            v2 = vel[2, l] + courant * (jnp.where(lane == 127, 0.0, pltpu.roll(here, 127, 1)) - here)
            vel[2, l] = v2
            flux = buoy[l + 1] * v2
            total[l] = part + (flux - jnp.where(lane == 0, 0.0, pltpu.roll(flux, 1, 1)))
            return 0

        lax.fori_loop(0, 4, inner, 0)

        def inner_x(l, _):
            v = vel[0, l] + courant * (load[l + 1, 0:256] - load[l, 0:256])
            vel[0, l] = v
            fx[l] = buoy[l + 1] * v
            return 0

        lax.fori_loop(0, 3, inner_x, 0)
        if n == 0:
            for copy in halo_x:
                copy.wait_recv()
            buoy[0] = hs[1].astype(F32) * has_below
        v = vxm[...] + courant * load[0, 0:256]
        vxm[...] = v
        pres[0] = pres[0] + courant * (total[0] + (fx[0] - buoy[0] * v))
        v = vel[0, 3] - courant * load[3, 0:256]
        vel[0, 3] = v
        pres[3] = pres[3] + courant * (total[3] + (buoy[4] * v - fx[2]))

        def middle(l, _):
            pres[l] = pres[l] + courant * (total[l] + (fx[l] - fx[l - 1]))
            return 0

        lax.fori_loop(1, 3, middle, 0)
        if n < 3:
            add_source(n + 1)
            ready = packed(load_part)
        exchanges(f"inner{n}")

        if n == 0:
            for copy in halo_z:
                copy.wait_recv()
        for copy in copies_z:
            copy.wait_recv()
        exchanges(f"third{n}")
        past = hz[n, 1] * has_z_above
        before_v = vzm[...] + courant * (zs[n, 1] - hz[n, 0])
        vzm[...] = before_v
        before = hc[0:8] / hc[8:16] * before_v * has_z_below
        rows = jnp.concatenate(
            [rounded(past), past - rounded(past), rounded(before), before - rounded(before)], 0)
        columns = jnp.transpose(rows).astype(BF16)
        for j in (0, 1, 6, 7):
            spread(columns, j)
        for k, l in enumerate((0, 3)):
            shares[k] = rim_share(l)

        for copy in copies_x:
            copy.wait_recv()
        below_x = hx[n, 0].astype(F32)
        vxm[...] = vxm[...] - courant * below_x
        share_0 = courant * courant * buoy[0] * below_x
        dv = courant * has_above * hx[n, 1].astype(F32)
        vel[0, 3] = vel[0, 3] + dv
        share_3 = courant * buoy[4] * dv
        for k, (l, share) in enumerate(((0, share_0), (3, share_3))):
            whole = shares[k] + share
            pres[l] = pres[l] + whole
            if n < 3:
                owed[k] = (stiff[l] * share).astype(BF16)
                now = load[l, 0:256] + stiff[l] * whole
                load[l, 0:256] = now
                sx[n + 1, 1 - k] = now.astype(BF16)
        if n < 3:
            copies_x = send_halos(n + 1, (sx, hx), (x_send, x_recv), x_to)
            ready = ready + packed(owed_part, (0, 1, 6, 7))
            zs[n + 1, 0] = ready[8:16] + courant * courant * zo[8:16] * zo[8:16] * past
            zs[n + 1, 1] = ready[0:8] - courant * zo[0:8] * zo[16:24] * before
            copies_z = send_halos(n + 1, (zs, hz), (z_send, z_recv), z_to)
        for j in (2, 3, 4, 5):
            spread(columns, j)

        def rest(l, _):
            share = rim_share(l)
            pres[l] = pres[l] + share
            if n < 3:
                load[l, 0:256] = load[l, 0:256] + stiff[l] * share
            return 0

        lax.fori_loop(1, 3, rest, 0)

    for copy in sent:
        copy.wait_send()
    pltpu.make_async_copy(acc.at[:, 0:32 * 31], acc.at[:, 0:32 * 31], send).wait()


def flush(pres, vel, pres_out, vel_out, sem):
    copies = [pltpu.make_async_copy(vel.at[d], vel_out.at[d], sem.at[d]) for d in range(3)]
    copies.append(pltpu.make_async_copy(pres, pres_out, sem.at[3]))
    for copy in copies:
        copy.start()
    for copy in copies:
        copy.wait()


def on_device(source, speed, impedance):
    vmem = pl.BlockSpec(memory_space=pltpu.VMEM)
    hbm = pl.BlockSpec(memory_space=pltpu.HBM)
    dma = pltpu.SemaphoreType.DMA
    held = pl.pallas_call(
        kernel,
        out_shape=(
            jax.ShapeDtypeStruct((4, 256, 128), F32),
            jax.ShapeDtypeStruct((3, 4, 256, 128), F32),
        ),
        in_specs=[hbm, hbm, hbm],
        out_specs=(vmem, vmem),
        scratch_shapes=[
            pltpu.VMEM((4, 1024, 128), BF16),
            pltpu.VMEM((4, 256, 128), BF16),
            pltpu.VMEM((4, 256, 128), BF16),
            pltpu.VMEM((2, 256, 128), BF16),
            pltpu.VMEM((4, 2, 256, 128), BF16),
            pltpu.VMEM((4, 2, 256, 128), BF16),
            pltpu.VMEM((16, 128), F32),
            pltpu.VMEM((16, 128), F32),
            pltpu.VMEM((4, 2, 8, 128), F32),
            pltpu.VMEM((4, 2, 8, 128), F32),
            pltpu.VMEM((4, 256, 128), F32),
            pltpu.VMEM((5, 256, 128), F32),
            pltpu.VMEM((256, 128), F32),
            pltpu.VMEM((3, 256, 128), F32),
            pltpu.VMEM((4, 264, 128), F32),
            pltpu.VMEM((264, 128), F32),
            pltpu.VMEM((4, 256, 128), F32),
            pltpu.VMEM((4, 256, 128), F32),
            pltpu.VMEM((8, 128), F32),
            pltpu.VMEM((2, 256, 128), BF16),
            pltpu.VMEM((2, 256, 128), F32),
            pltpu.VMEM((32, 128), F32),
            dma, dma((4, 2)), dma((3,)), dma, dma, dma, dma,
            dma((4, 2)), dma((4, 2)), dma((4, 2)), dma((4, 2)),
        ],
        compiler_params=pltpu.CompilerParams(
            collective_id=0, has_side_effects=True, vmem_limit_bytes=48 * 1024 * 1024),
    )(*(pltpu.with_memory_space_constraint(a, pltpu.HBM) for a in (source.reshape(4, 1024, 128), speed, impedance)))
    return pl.pallas_call(
        flush,
        out_shape=(
            jax.ShapeDtypeStruct((4, 256, 128), F32),
            jax.ShapeDtypeStruct((3, 4, 256, 128), F32),
        ),
        in_specs=[vmem, vmem],
        out_specs=(hbm, hbm),
        scratch_shapes=[dma((4,))],
        compiler_params=pltpu.CompilerParams(vmem_limit_bytes=8 * 1024 * 1024),
    )(*held)


def solution(mesh):
    in_specs = (
        P(None, None, ("grp", "gx"), "gy"),
        P(("grp", "gx"), None, "gy"),
        P(("grp", "gx"), None, "gy"),
    )
    out_specs = (P(("grp", "gx"), None, "gy"), P(None, ("grp", "gx"), None, "gy"))
    return jax.shard_map(on_device, mesh=mesh, in_specs=in_specs, out_specs=out_specs, check_vma=False)
```
